256 devices in a mesh: fluid: 4 (over y), sx: 8 (over z), sy: 8 (over x, core).
Axes of the slice: x: 4, y: 4, z: 8, core: 2. Of those that a mesh axis runs over, the one named last changes fastest.
Arguments:
- opening_conductor_warmth: float32 [128, 128, 512], P('sx', 'sy', 'fluid'), may hold values from -19 to 19
- cellwise_diffusivity: float32 [128, 128, 512], P('sx', 'sy', 'fluid'), may hold values from 0.15 to 1
- previous_thermal_states: float32 [56, 128, 128, 512], P(None, 'sx', 'sy', 'fluid'), may hold values from -19 to 19
- boundary_heat_rate_pieces: float32 [1048576, 128], P(('fluid', 'sx', 'sy')), may hold values from -6 to 6
- receiving_processor_per_piece: int32 [1048576, 1], P(('fluid', 'sx', 'sy')), may hold values from 0 to 255; in each aligned block of 4096 rows (0 to 4095, 4096 to 8191, ...) at most 32 rows name the same one
- boundary_line_position_in_tile: int32 [1048576, 1], P(('fluid', 'sx', 'sy')), may hold values from 0 to 255
- piece_to_solid_line_mapping: float32 [128, 128], replicated, may hold values from -0.5 to 0.5
Outputs:
- field_out: float32 [128, 128, 512], P('sx', 'sy', 'fluid')
- inner_product_matrix: float32 [64, 64], P(('sx', 'sy'))
The draws below stay inside these ranges and needn't reach their ends.
Inputs may be any that keep to these rules, and one draw needn't show every extreme that they name: `receiving_processor_per_piece`: among one device's 4096 rows no device is named more than 32 times, and in every draw some device is named exactly 32 times by one device's rows.
All inputs are finite; a program needn't handle non-finite values.
Results may differ from the reference program's by a relative error of at most 0.000088.
Values sent between devices are 32-bit elements; how exact they have to be, the bound alone decides.
No kernel may reach another device: no remote copies, remote signals or barrier semaphores. Data moves between devices by JAX's collectives and lax.ppermute only.
A program may use at most 128 MiB of HBM per device.

```python
import math
import jax
import jax.numpy as jnp
import numpy as np
from jax import lax

CX = 16
CY = 16
CZ = 128
BLK = 128
K_DEV = 4096
STEPS = 8
HIST = 56
CAP = 32
LINES = 256
WALL = 1048576
NX = 128
NY = 128
NZ = 512
N_FLUID = 4
N_SX = 8
N_SY = 8
DEVICES = 256


def common_modes(key, spread):
    leading = jnp.clip(jax.random.normal(jax.random.fold_in(key, 101), (NX, NY, NZ), jnp.float32), -4.0, 4.0)
    trailing = jnp.clip(jax.random.normal(jax.random.fold_in(key, 102), (NX, NY, NZ), jnp.float32), -4.0, 4.0)
    spread_level = jax.random.uniform(jax.random.fold_in(key, 103), (NX, NY, NZ), jnp.float32)
    spread_log = math.log(spread)
    mean_square = (spread * spread - 1.0) / (2.0 * spread_log)
    amplitude = jnp.exp(spread_level * spread_log) / math.sqrt(mean_square)
    return (leading * amplitude, trailing * amplitude, amplitude)


def draw_previous_thermal_states(key, part):
    spread = 2.0
    leading, trailing, amplitude = common_modes(key, spread)
    key = jax.random.fold_in(key, 5)
    angles = 2.0 * (jnp.arange(HIST, dtype=jnp.float32) + 1.0) / HIST
    jitter = jnp.clip(jax.random.normal(key, (HIST, NX, NY, NZ), jnp.float32), -4.0, 4.0)
    cosines = jnp.cos(angles)[:, None, None, None]
    sines = jnp.sin(angles)[:, None, None, None]
    return cosines * leading[None] + sines * trailing[None] + 0.5 * jitter * amplitude[None]


def draw_opening_conductor_warmth(key, part):
    spread = 2.0
    leading, trailing, amplitude = common_modes(key, spread)
    key = jax.random.fold_in(key, 7)
    final_angle = 2.0 * (HIST + 1.0) / HIST
    jitter = jnp.clip(jax.random.normal(key, (NX, NY, NZ), jnp.float32), -4.0, 4.0)
    return math.cos(final_angle) * leading + math.sin(final_angle) * trailing + 0.5 * jitter * amplitude


def with_ends(array, rng, least, largest):
    longest = array.shape.index(max(array.shape))
    spots = []
    for shift in (0, 1):
        where = [jax.random.randint(jax.random.fold_in(rng, axis), (), 0, length) for axis, length in enumerate(array.shape)]
        where[longest] = (where[longest] + shift) % array.shape[longest]
        spots.append(tuple(where))
    return array.at[spots[0]].set(least).at[spots[1]].set(largest)


def levels(key, extent, pieces, least, largest):
    level = 1.0
    for axis_at, blocks in pieces:
        draws = jax.random.uniform(jax.random.fold_in(jax.random.fold_in(key, 6), axis_at), (blocks,), jnp.float32, least / len(pieces), largest / len(pieces))
        level = level * jnp.repeat(jnp.exp(draws), extent[axis_at] // blocks).reshape((-1,) + (1,) * (len(extent) - 1 - axis_at))
    return level


def routed_block(key, own, number, rows, count, top, bound, lean):
    ranking = jax.random.permutation(key, count)
    packed, usual = portions_of(count, rows * top, bound, lean, True), portions_of(count, rows * top, bound, lean, False)
    places = jnp.arange(count)

    def named(lengths, offset_by):
        used = int((lengths > 0).sum())
        fixed = max(1, used // 4)
        moved = fixed + (places - fixed + offset_by * (used - fixed)) % max(1, count - fixed)
        return jnp.zeros((count,), jnp.int32).at[ranking[jnp.where(places < fixed, places, moved)]].set(jnp.asarray(lengths, jnp.int32))

    lengths = jnp.where(number % 4 == 0, named(packed, number // 4), named(usual, number - number // 4 - 1))
    mixed = jax.random.permutation(jax.random.fold_in(own, 3), count)
    source_of, receiver = mixed[0:count // 2 * 2:2], mixed[1:count // 2 * 2:2]
    margin = jnp.minimum(lengths[source_of] - 1, bound - lengths[receiver]) // 2
    margin = jnp.where((source_of == ranking[0]) | (receiver == ranking[0]) | (lengths[receiver] == 0), 0, jnp.maximum(margin, 0))
    moved = jax.random.randint(jax.random.fold_in(own, 4), (count // 2,), 0, 1 << 20) % (margin + 1)
    lengths = lengths.at[source_of].add(-moved).at[receiver].add(moved)
    items = jnp.searchsorted(jnp.cumsum(lengths), jnp.arange(rows * top), side="right").astype(jnp.int32)
    table = items.reshape(top, rows).T
    table = table[jax.random.permutation(jax.random.fold_in(own, 1), rows)]
    offset_by = jax.random.randint(jax.random.fold_in(own, 2), (rows, 1), 0, top)
    return jnp.take_along_axis(table, (jnp.arange(top)[None, :] + offset_by) % top, axis=1)


def portions_of(amount, total, limit, lean, full):
    weights = [(1 << 20) // math.isqrt(standing ** lean) + 1 for standing in range(1, amount + 1)]
    largest = limit if full else min(limit, max(-(-total // amount), total * weights[0] // sum(weights)))
    least = 1 if total - largest >= amount - 1 else 0
    holding, rest = [largest] + [least] * (amount - 1), total - largest - least * (amount - 1)
    while rest > 0:
        movable = [i for i in range(1, amount) if holding[i] < largest] or [i for i in range(1, amount) if holding[i] < limit]
        whole, remaining = sum([weights[i] for i in movable]), rest
        for i in movable:
            more = min(limit - holding[i], max(1, remaining * weights[i] // whole), rest)
            holding[i] = holding[i] + more
            rest = rest - more
    return np.array(holding)


def normal_values(own_key, shape, scale, limit, pieces=(), kind=jnp.bfloat16):
    array = jax.random.normal(own_key, shape, jnp.float32) * scale
    if len(pieces) > 0:
        array = levels(own_key, shape, pieces, -0.22, 0.18) * array
    return jnp.clip(array, min=-limit, max=limit).astype(kind)


def setup_inputs(seed: int = 0) -> dict:
    keys = jax.random.split(jax.random.key(seed), 8)
    opening_conductor_warmth = draw_opening_conductor_warmth(jax.random.fold_in(keys[7], 71), 0)
    cellwise_diffusivity = jnp.clip(jnp.exp(math.log(1.0) - 1.89712 * jax.random.uniform(keys[1], (NX, NY, NZ), jnp.float32) ** levels(keys[1], (NX, NY, NZ), ((0, 8), (1, 8), (2, 4)), -0.2, 0.2)), 0.15, 1.0)
    previous_thermal_states = draw_previous_thermal_states(jax.random.fold_in(keys[7], 71), 0)
    boundary_heat_rate_pieces = normal_values(keys[3], (WALL, BLK), 1.0, 6.0, ((0, 256),), jnp.float32)
    receiving_processor_per_piece_keys = jax.random.split(jax.random.fold_in(keys[4], 1), WALL // K_DEV)
    receiving_processor_per_piece_turns = jax.random.permutation(jax.random.fold_in(keys[4], 3), WALL // K_DEV)
    receiving_processor_per_piece = jax.vmap(lambda own, number: routed_block(jax.random.fold_in(keys[4], 2), own, number, K_DEV, DEVICES, 1, CAP, 2))(receiving_processor_per_piece_keys, receiving_processor_per_piece_turns).reshape((WALL, 1))
    boundary_line_position_in_tile = with_ends(jax.random.randint(keys[5], (WALL, 1), 0, LINES), jax.random.fold_in(keys[5], 1), 0, LINES - 1).astype(jnp.int32)
    piece_to_solid_line_mapping = normal_values(keys[6], (BLK, CZ), BLK ** -0.5, 0.5, (), jnp.float32)
    return dict(opening_conductor_warmth=opening_conductor_warmth, cellwise_diffusivity=cellwise_diffusivity, previous_thermal_states=previous_thermal_states, boundary_heat_rate_pieces=boundary_heat_rate_pieces, receiving_processor_per_piece=receiving_processor_per_piece, boundary_line_position_in_tile=boundary_line_position_in_tile, piece_to_solid_line_mapping=piece_to_solid_line_mapping)


rate_step = 0.16
source_gain = 0.1


def increment_change(margin_extended_grid, cellwise_diffusivity, deposited_energy):
    center = margin_extended_grid[1:-1, 1:-1, 1:-1]
    beside = margin_extended_grid[2:, 1:-1, 1:-1] + margin_extended_grid[:-2, 1:-1, 1:-1]
    beside = beside + margin_extended_grid[1:-1, 2:, 1:-1] + margin_extended_grid[1:-1, :-2, 1:-1]
    beside = beside + margin_extended_grid[1:-1, 1:-1, 2:] + margin_extended_grid[1:-1, 1:-1, :-2]
    return center + rate_step * cellwise_diffusivity * (beside - 6.0 * center) + deposited_energy


def reference(opening_conductor_warmth, cellwise_diffusivity, previous_thermal_states, boundary_heat_rate_pieces, receiving_processor_per_piece, boundary_line_position_in_tile, piece_to_solid_line_mapping):
    lines = jnp.dot(boundary_heat_rate_pieces, piece_to_solid_line_mapping, precision=lax.Precision.HIGHEST, preferred_element_type=jnp.float32)
    target = receiving_processor_per_piece[:, 0].astype(jnp.int32) * LINES + boundary_line_position_in_tile[:, 0].astype(jnp.int32)
    deposit = jax.ops.segment_sum(lines, target, num_segments=DEVICES * LINES)
    deposit = deposit.reshape(N_FLUID, N_SX, N_SY, CX, CY, CZ).transpose(1, 3, 2, 4, 0, 5).reshape(NX, NY, NZ)
    deposited_energy = source_gain * deposit
    existing_conductor_warmth = opening_conductor_warmth
    recorded_frames = []
    for step_index in range(STEPS):
        existing_conductor_warmth = increment_change(jnp.pad(existing_conductor_warmth, 1), cellwise_diffusivity, deposited_energy)
        recorded_frames.append(existing_conductor_warmth)
    new_rows = jnp.stack(recorded_frames).reshape(STEPS, -1)
    snapshot_history_rows = previous_thermal_states.reshape(HIST, -1)
    cells = float(NX * NY * NZ)
    upper_left = jnp.dot(snapshot_history_rows, snapshot_history_rows.T, precision=lax.Precision.HIGHEST, preferred_element_type=jnp.float32)
    upper_right = jnp.dot(snapshot_history_rows, new_rows.T, precision=lax.Precision.HIGHEST, preferred_element_type=jnp.float32)
    lower_right = jnp.dot(new_rows, new_rows.T, precision=lax.Precision.HIGHEST, preferred_element_type=jnp.float32)
    inner_product_matrix = jnp.concatenate([jnp.concatenate([upper_left, upper_right], 1), jnp.concatenate([upper_right.T, lower_right], 1)], 0) / cells
    return existing_conductor_warmth, inner_product_matrix
```

```python
import functools

import jax
import jax.numpy as jnp
from jax import lax
from jax.experimental import pallas as pl
from jax.experimental.pallas import tpu as pltpu
from jax.sharding import Mesh
from jax.sharding import PartitionSpec as P

STEPS = 8
HALO = 8
HIST = 56
SNAPS = HIST + STEPS
SLOTS = 32
LINES = 256
LANES = 128
QUADS = 4
PEERS = 64
PEER_ROWS = QUADS * SLOTS + 8
CHUNK = 256
TILE = 16
WIDE = TILE + 2 * HALO

rate_step = 0.16
source_gain = 0.1

SX = ("sxq", "sxp")
PLANE = ("fluid", "sxp", "sy")
ALL = ("fluid", "sxq", "sxp", "sy")

f32 = jnp.float32
bf16 = jnp.bfloat16


def dot_nt(a, b, precision=None):
    return lax.dot_general(
        a, b, (((1,), (1,)), ((), ())), precision=precision, preferred_element_type=f32
    )


def split(x):
    high = x.astype(bf16)
    return high, (x - high.astype(f32)).astype(bf16)


def rank_kernel(shift_ref, owner_ref, line_ref, slot_ref, label_ref, carry_ref):
    carry_ref[...] = jnp.zeros_like(carry_ref)
    label_ref[...] = jnp.zeros_like(label_ref)
    rows = lax.broadcasted_iota(jnp.int32, (CHUNK, CHUNK), 0)
    cols = lax.broadcasted_iota(jnp.int32, (CHUNK, CHUNK), 1)
    earlier = jnp.where(rows < cols, 1.0, 0.0).astype(bf16)
    places = lax.broadcasted_iota(jnp.int32, (LANES, CHUNK), 0)
    shift = shift_ref[0]

    def body(c, _):
        owner = owner_ref[pl.ds(c, 1), :]
        fluid, sx, sy = owner >> 6, (owner >> 3) & 7, owner & 7
        peer = (fluid * 2 + (sx & 1)) * 8 + sy
        quad = sx >> 1
        match = rows == peer * QUADS + quad
        hit = jnp.where(match, 1.0, 0.0)
        hit16 = hit.astype(bf16)
        before = jnp.dot(hit16, earlier, preferred_element_type=f32)
        rank = jnp.sum(jnp.where(match, before + carry_ref[...], 0.0), axis=0, keepdims=True)
        carry_ref[...] += before[:, CHUNK - 1 :] + hit[:, CHUNK - 1 :]
        rank = rank.astype(jnp.int32)
        slot_ref[pl.ds(c, 1), :] = peer * PEER_ROWS + quad * SLOTS + rank
        value = (line_ref[pl.ds(c, 1), :] + 1).astype(f32)
        spread = jnp.where(places == rank + shift, value, 0.0).astype(bf16)
        label_ref[...] += dot_nt(hit16, spread)
        return 0

    lax.fori_loop(0, owner_ref.shape[0], body, 0)


def pack_kernel(slot_ref, blocks_ref, label_ref, out_ref):
    def clear(i, _):
        out_ref[pl.ds(pl.multiple_of(i * PEER_ROWS, 8), PEER_ROWS), :] = jnp.zeros(
            (PEER_ROWS, LANES), f32
        )
        return 0

    lax.fori_loop(0, PEERS, clear, 0)
    for h in range(PEERS // 2):
        for e in range(2):
            at = (2 * h + e) * PEER_ROWS + QUADS * SLOTS
            out_ref[at : at + QUADS, :] = label_ref[8 * h + 4 * e : 8 * h + 4 * e + 4, :]

    step = 32
    per_row = slot_ref.shape[1] // step

    def place(i, _):
        row, col = i // per_row, (i % per_row) * step
        for t in range(step):
            slot = slot_ref[row, col + t]
            out_ref[pl.ds(slot, 1), :] = blocks_ref[pl.ds(i * step + t, 1), :]
        return 0

    lax.fori_loop(0, blocks_ref.shape[0] // step, place, 0)


def deposit_kernel(quad_ref, block_ref, map_ref, *rest):
    outs, total = rest[:QUADS], rest[QUADS]
    g = pl.program_id(0)

    @pl.when(g == 0)
    def _():
        total[...] = jnp.zeros_like(total)

    lines = lax.broadcasted_iota(jnp.int32, (LINES, LANES), 0).astype(f32) + 1.0
    for q in range(QUADS):
        marks = []
        for half in range(2):
            at = QUADS * SLOTS + q
            label = block_ref[4 * half, at : at + 1, :]
            for t in range(1, 4):
                label = label + block_ref[4 * half + t, at : at + 1, :]
            marks.append(jnp.where(lines == label, 1.0, 0.0).astype(bf16))
        mark = jnp.concatenate(marks, axis=1)
        values = block_ref[:, q * SLOTS : (q + 1) * SLOTS, :].reshape(8 * SLOTS, LANES)
        high, low = split(values)
        total[q] += jnp.dot(
            mark, jnp.concatenate([high, low], axis=1), preferred_element_type=f32
        )

    @pl.when(g == pl.num_programs(0) - 1)
    def _():
        for k in range(QUADS):
            both = total[(quad_ref[0] + k) % QUADS]
            outs[k][...] = source_gain * jnp.dot(
                both[:, :LANES] + both[:, LANES:],
                map_ref[...],
                precision=lax.Precision.HIGHEST,
                preferred_element_type=f32,
            )


def step_kernel(
    start_ref,
    source_ref,
    source_up,
    source_down,
    source_left,
    source_right,
    past_gram,
    history,
    field_ref,
    rows_ref,
    now_m,
    now_e,
    next_m,
    next_e,
    src_m,
    src_e,
    snaps,
    past,
    acc,
    sem,
):
    load = pltpu.make_async_copy(history, past, sem)
    load.start()
    pad = WIDE
    count = WIDE * WIDE
    for k, (now, src) in enumerate(((now_m, src_m), (now_e, src_e))):
        now[0:pad, :] = jnp.zeros((pad, LANES), f32)
        now[pad + count :, :] = jnp.zeros((pad, LANES), f32)
        now[pad : pad + count, :] = start_ref[2 * k]
        for x in range(WIDE):
            src[x * WIDE : x * WIDE + HALO, :] = source_left[k, x]
            src[x * WIDE + WIDE - HALO : (x + 1) * WIDE, :] = source_right[k, x]
            if x < HALO:
                middle = source_up[k, x]
            elif x < HALO + TILE:
                middle = source_ref[k, x - HALO]
            else:
                middle = source_down[k, x - HALO - TILE]
            src[x * WIDE + HALO : x * WIDE + HALO + TILE, :] = middle
    lane = lax.broadcasted_iota(jnp.int32, (WIDE, LANES), 1)
    first, last = lane == 0, lane == LANES - 1

    def advance(a_m, a_e, b_m, b_e, s):
        def body(x, _):
            r = pl.multiple_of(x * WIDE, 8)
            at = lambda off: pl.ds(r + pad + off, WIDE)
            own = pl.ds(r, WIDE)
            m, e = a_m[at(0), :], a_e[at(0), :]
            roll = lambda v, d: pltpu.roll(v, d % LANES, 1)
            mr, er, ml, el = roll(m, 1), roll(e, 1), roll(m, -1), roll(e, -1)
            sides = (
                (a_m, b_m, m, jnp.where(first, er, mr) + jnp.where(last, el, ml), 1, src_m),
                (a_e, b_e, e, jnp.where(first, mr, er) + jnp.where(last, ml, el), 3, src_e),
            )
            for a, b, v, beside, d, src in sides:
                beside = beside + (a[at(-WIDE), :] + a[at(WIDE), :])
                beside = beside + (a[at(-1), :] + a[at(1), :])
                b[at(0), :] = v + start_ref[d, own, :] * (beside - 6.0 * v) + src[own, :]
            return 0

        lax.fori_loop(s + 1, WIDE - 1 - s, body, 0)
        for x in range(TILE):
            r = pad + (x + HALO) * WIDE + HALO
            for h in range(2):
                snaps[x * 2 + h, 8 * s : 8 * s + 8, :] = b_m[r + 8 * h : r + 8 * h + 8, :]

    for s in range(0, STEPS, 2):
        if s == 0:
            next_m[...] = jnp.zeros_like(next_m)
            next_e[...] = jnp.zeros_like(next_e)
        advance(now_m, now_e, next_m, next_e, s)
        advance(next_m, next_e, now_m, now_e, s + 1)
    for x in range(TILE):
        for h in range(2):
            field_ref[x, 8 * h : 8 * h + 8, :] = snaps[x * 2 + h, 8 * (STEPS - 1) :, :]

    load.wait()
    acc[...] = jnp.zeros_like(acc)
    tall = 8 * HIST

    def gram(i, _):
        x, h = (i // 2) * 2, i % 2
        new = [snaps[(x + e) * 2 + h] for e in range(2)]
        old = [
            past[:, x + e, pl.ds(pl.multiple_of(h * 8, 8), 8), :].reshape(tall, LANES)
            for e in range(2)
        ]
        new_high, new_low = split(jnp.concatenate(new, axis=1))
        old_high, old_low = split(jnp.concatenate(old, axis=1))
        right = jnp.concatenate([new_high, new_low], axis=0)
        acc[0:tall, :] += dot_nt(old_high, right) + dot_nt(old_low, right)
        acc[tall:, :] += dot_nt(new_high, right) + dot_nt(new_low, right)
        return 0

    lax.fori_loop(0, TILE, gram, 0)
    y = lax.broadcasted_iota(jnp.int32, acc.shape, 0) % 8
    y_new = lax.broadcasted_iota(jnp.int32, acc.shape, 1) % 8
    products = jnp.where(y == y_new, acc[...], 0.0).reshape(SNAPS, 8, 2 * 8 * STEPS).sum(axis=1)
    snap_of = lambda shape, dim: (lax.broadcasted_iota(jnp.int32, shape, dim) % 64) // 8
    wide, tallest = (2 * 8 * STEPS, SNAPS), (STEPS, 2 * 8 * STEPS)
    pick = snap_of(wide, 0) == lax.broadcasted_iota(jnp.int32, wide, 1) - HIST
    right = jnp.dot(
        products,
        jnp.where(pick, 1.0, 0.0),
        precision=lax.Precision.HIGHEST,
        preferred_element_type=f32,
    )
    pick = snap_of(tallest, 1) == lax.broadcasted_iota(jnp.int32, tallest, 0)
    low = dot_nt(jnp.where(pick, 1.0, 0.0), products, lax.Precision.HIGHEST)
    upper = past_gram[...] + right[:HIST]
    for f in range(rows_ref.shape[0] // SNAPS):
        rows_ref[f * SNAPS : f * SNAPS + HIST, :] = upper
        rows_ref[f * SNAPS + HIST : (f + 1) * SNAPS, :] = low


def up_chain(axis):
    count = lax.axis_size(axis)
    return [(i, i + 1) for i in range(count - 1)]


def down_chain(axis):
    count = lax.axis_size(axis)
    return [(i + 1, i) for i in range(count - 1)]


def beyond(cells):
    after = lax.ppermute(cells, "fluid", down_chain("fluid"))
    before = lax.ppermute(cells, "fluid", up_chain("fluid"))
    lane = lax.broadcasted_iota(jnp.int32, cells.shape, cells.ndim - 1)
    return jnp.where(lane < LANES // 2, after, before)


def slabs(cells):
    up = lax.ppermute(cells[:, TILE - HALO :], SX, up_chain(SX))
    down = lax.ppermute(cells[:, :HALO], SX, down_chain(SX))
    tall = jnp.concatenate([up, cells, down], axis=1)
    left = lax.ppermute(tall[:, :, TILE - HALO :], "sy", up_chain("sy"))
    right = lax.ppermute(tall[:, :, :HALO], "sy", down_chain("sy"))
    return up, down, tall, left, right


def whole(shape):
    return pl.BlockSpec(shape, lambda *_: (0,) * len(shape))


def local(
    opening_conductor_warmth,
    cellwise_diffusivity,
    previous_thermal_states,
    boundary_heat_rate_pieces,
    receiving_processor_per_piece,
    boundary_line_position_in_tile,
    piece_to_solid_line_mapping,
):
    blocks = boundary_heat_rate_pieces.shape[0]
    chunks = blocks // CHUNK
    vmem = pl.BlockSpec(memory_space=pltpu.VMEM)
    smem = pl.BlockSpec(memory_space=pltpu.SMEM)
    limit = pltpu.CompilerParams(vmem_limit_bytes=48 * 1024 * 1024)

    with jax.named_scope("rank"):
        shift = (lax.axis_index("sy") % 4 * SLOTS).astype(jnp.int32).reshape(1)
        slots, labels = pl.pallas_call(
            rank_kernel,
            out_shape=(
                jax.ShapeDtypeStruct((chunks, CHUNK), jnp.int32),
                jax.ShapeDtypeStruct((CHUNK, LANES), f32),
            ),
            in_specs=[smem, vmem, vmem],
            out_specs=(vmem, vmem),
            scratch_shapes=[pltpu.VMEM((CHUNK, 1), f32)],
            compiler_params=limit,
        )(
            shift,
            receiving_processor_per_piece.reshape(chunks, CHUNK),
            boundary_line_position_in_tile.reshape(chunks, CHUNK),
        )

    with jax.named_scope("pack"):
        packed = pl.pallas_call(
            pack_kernel,
            out_shape=jax.ShapeDtypeStruct((PEERS * PEER_ROWS, LANES), f32),
            in_specs=[smem, vmem, vmem],
            out_specs=vmem,
            compiler_params=limit,
        )(slots, boundary_heat_rate_pieces, labels)

    with jax.named_scope("early_halo"):
        pair = jnp.stack([opening_conductor_warmth, rate_step * cellwise_diffusivity])
        pair = jnp.concatenate([pair, beyond(pair)])
        _, _, tall, left, right = slabs(pair)
        start = jnp.concatenate([left, tall, right], axis=2).reshape(4, WIDE * WIDE, LANES)
        packed, start = lax.optimization_barrier((packed, start))

    with jax.named_scope("exchange"):
        received = lax.all_to_all(
            packed.reshape(PEERS, PEER_ROWS, LANES), PLANE, split_axis=0, concat_axis=0, tiled=True
        )

    with jax.named_scope("history"):
        flat = previous_thermal_states.reshape(HIST, -1)
        cells = float(flat.shape[1] * lax.axis_size(ALL))
        past_gram = jnp.dot(
            flat, flat.T, precision=lax.Precision.HIGHEST, preferred_element_type=f32
        )
        past_gram = jnp.pad(past_gram, ((0, 0), (0, STEPS)))

    with jax.named_scope("deposit"):
        part = jax.ShapeDtypeStruct((LINES, LANES), f32)
        parts = pl.pallas_call(
            deposit_kernel,
            out_shape=(part,) * QUADS,
            grid_spec=pltpu.PrefetchScalarGridSpec(
                num_scalar_prefetch=1,
                grid=(PEERS // 8,),
                in_specs=[
                    pl.BlockSpec((8, PEER_ROWS, LANES), lambda g, _: (g, 0, 0)),
                    whole((LANES, LANES)),
                ],
                out_specs=(whole((LINES, LANES)),) * QUADS,
                scratch_shapes=[pltpu.VMEM((QUADS, LINES, 2 * LANES), f32)],
            ),
            compiler_params=limit,
        )(lax.axis_index("sxq").astype(jnp.int32).reshape(1), received, piece_to_solid_line_mapping)
        source = parts[0]
        for k in range(1, QUADS):
            ring = [(i, (i + k) % QUADS) for i in range(QUADS)]
            source = source + lax.ppermute(parts[k], "sxq", ring)
        source = source.reshape(1, TILE, TILE, LANES)

    with jax.named_scope("source_halo"):
        source = jnp.concatenate([source, beyond(source)])
        up, down, _, left, right = slabs(source)

    with jax.named_scope("steps"):
        rows = lax.axis_size("fluid") * SNAPS
        grid_rows = WIDE * WIDE
        buffer = pltpu.VMEM((grid_rows + 2 * WIDE, LANES), f32)
        field, gram_rows = pl.pallas_call(
            step_kernel,
            out_shape=(
                jax.ShapeDtypeStruct((TILE, TILE, LANES), f32),
                jax.ShapeDtypeStruct((rows, SNAPS), f32),
            ),
            in_specs=[vmem] * 7 + [pl.BlockSpec(memory_space=pl.ANY)],
            out_specs=(vmem, vmem),
            scratch_shapes=[
                buffer,
                buffer,
                buffer,
                buffer,
                pltpu.VMEM((grid_rows, LANES), f32),
                pltpu.VMEM((grid_rows, LANES), f32),
                pltpu.VMEM((TILE * 2, 8 * STEPS, LANES), f32),
                pltpu.VMEM((HIST, TILE, TILE, LANES), f32),
                pltpu.VMEM((8 * SNAPS, 2 * 8 * STEPS), f32),
                pltpu.SemaphoreType.DMA,
            ],
            compiler_params=limit,
        )(start, source, up, down, left, right, past_gram, previous_thermal_states)

    with jax.named_scope("gram_sum"):
        shares = lax.all_to_all(gram_rows, ALL, split_axis=0, concat_axis=0, tiled=True)
        inner_product_matrix = jnp.sum(shares, axis=0, keepdims=True) / cells
    return field, inner_product_matrix


def solution(mesh):
    fluid, sx, sy = (mesh.shape[name] for name in ("fluid", "sx", "sy"))
    inner = Mesh(mesh.devices.reshape(fluid, sx // 2, 2, sy), ALL)
    cell = P(SX, "sy", "fluid")
    wall = P(ALL, None)
    return jax.shard_map(
        local,
        mesh=inner,
        in_specs=(cell, cell, P(None, SX, "sy", "fluid"), wall, wall, wall, P()),
        out_specs=(cell, P((*SX, "sy"), None)),
        check_vma=False,
    )
```

```python
import functools

import jax
import jax.numpy as jnp
from jax import lax
from jax.experimental import pallas as pl
from jax.experimental.pallas import tpu as pltpu
from jax.sharding import Mesh
from jax.sharding import PartitionSpec as P

STEPS = 8
HALO = 8
HIST = 56
SNAPS = HIST + STEPS
SLOTS = 32
LINES = 256
LANES = 128
QUADS = 4
PEERS = 64
PEER_ROWS = QUADS * SLOTS + 8
CHUNK = 256
TILE = 16
WIDE = TILE + 2 * HALO

rate_step = 0.16
source_gain = 0.1

SX = ("sxq", "sxp")
PLANE = ("fluid", "sxp", "sy")
ALL = ("fluid", "sxq", "sxp", "sy")

f32 = jnp.float32
bf16 = jnp.bfloat16


def dot_nt(a, b, precision=None):
    return lax.dot_general(
        a, b, (((1,), (1,)), ((), ())), precision=precision, preferred_element_type=f32
    )


def split(x):
    high = x.astype(bf16)
    return high, (x - high.astype(f32)).astype(bf16)


def rank_kernel(shift_ref, owner_ref, line_ref, slot_ref, label_ref):
    rows = lax.broadcasted_iota(jnp.int32, (CHUNK, CHUNK), 0)
    cols = lax.broadcasted_iota(jnp.int32, (CHUNK, CHUNK), 1)
    earlier = jnp.where(rows < cols, 1.0, 0.0).astype(bf16)
    places = lax.broadcasted_iota(jnp.int32, (LANES, CHUNK), 0)
    shift = shift_ref[0]
    carry = jnp.zeros((CHUNK, 1), f32)
    labels = jnp.zeros((CHUNK, LANES), f32)
    for c in range(0, owner_ref.shape[1], CHUNK):
        owner = owner_ref[:, c : c + CHUNK]
        fluid, sx, sy = owner >> 6, (owner >> 3) & 7, owner & 7
        peer = (fluid * 2 + (sx & 1)) * 8 + sy
        quad = sx >> 1
        match = rows == peer * QUADS + quad
        hit = jnp.where(match, 1.0, 0.0)
        hit16 = hit.astype(bf16)
        before = jnp.dot(hit16, earlier, preferred_element_type=f32)
        rank = jnp.sum(jnp.where(match, before + carry, 0.0), axis=0, keepdims=True)
        carry = carry + (before[:, CHUNK - 1 :] + hit[:, CHUNK - 1 :])
        rank = rank.astype(jnp.int32)
        slot_ref[:, c : c + CHUNK] = peer * PEER_ROWS + quad * SLOTS + rank
        value = (line_ref[:, c : c + CHUNK] + 1).astype(f32)
        spread = jnp.where(places == rank + shift, value, 0.0).astype(bf16)
        labels = labels + dot_nt(hit16, spread)
    label_ref[...] = labels


def pack_kernel(slot_ref, blocks_ref, label_ref, out_ref):
    def clear(i, _):
        out_ref[pl.ds(pl.multiple_of(i * PEER_ROWS, 8), PEER_ROWS), :] = jnp.zeros(
            (PEER_ROWS, LANES), f32
        )
        return 0

    lax.fori_loop(0, PEERS, clear, 0)
    for h in range(PEERS // 2):
        for e in range(2):
            at = (2 * h + e) * PEER_ROWS + QUADS * SLOTS
            out_ref[at : at + QUADS, :] = label_ref[8 * h + 4 * e : 8 * h + 4 * e + 4, :]

    step = 64

    def place(i, _):
        base = pl.multiple_of(i * step, step)
        for t in range(step):
            out_ref[pl.ds(slot_ref[0, base + t], 1), :] = blocks_ref[pl.ds(base + t, 1), :]
        return 0

    lax.fori_loop(0, blocks_ref.shape[0] // step, place, 0)


def deposit_kernel(ahead, quad_ref, block_ref, label_ref, map_ref, out_ref):
    quad = (quad_ref[0] + ahead) % QUADS
    lines = lax.broadcasted_iota(jnp.int32, (LINES, LANES), 0).astype(f32) + 1.0
    labels = label_ref[:, pl.ds(quad, 1), :].reshape(PEERS // 4, 4, LANES).sum(axis=1)
    total = jnp.zeros((LINES, 2 * LANES), f32)
    for g in range(PEERS // 8):
        marks = [
            jnp.where(lines == labels[h : h + 1], 1.0, 0.0).astype(bf16)
            for h in (2 * g, 2 * g + 1)
        ]
        high, low = split(block_ref[8 * g : 8 * g + 8].reshape(8 * SLOTS, LANES))
        total = total + jnp.dot(
            jnp.concatenate(marks, axis=1),
            jnp.concatenate([high, low], axis=1),
            preferred_element_type=f32,
        )
    high, low = split(total[:, :LANES] + total[:, LANES:])
    map_high, map_low = split(map_ref[...])
    both = jnp.concatenate([map_high, map_low], axis=1)
    once = jnp.concatenate([map_high, jnp.zeros_like(map_low)], axis=1)
    mapped = jnp.dot(
        jnp.concatenate([high, low], axis=1),
        jnp.concatenate([both, once], axis=0),
        preferred_element_type=f32,
    )
    out_ref[...] = source_gain * (mapped[:, :LANES] + mapped[:, LANES:])


def step_kernel(
    start_ref,
    source_ref,
    source_up,
    source_down,
    source_left,
    source_right,
    past_gram,
    history,
    field_ref,
    rows_ref,
    now_m,
    now_e,
    next_m,
    next_e,
    src_m,
    src_e,
    snaps,
    past,
    acc,
    sem,
):
    load = pltpu.make_async_copy(history, past, sem)
    load.start()
    pad = WIDE
    count = WIDE * WIDE
    for k, (now, src) in enumerate(((now_m, src_m), (now_e, src_e))):
        now[0:pad, :] = jnp.zeros((pad, LANES), f32)
        now[pad + count :, :] = jnp.zeros((pad, LANES), f32)
        now[pad : pad + count, :] = start_ref[2 * k]
        for x in range(WIDE):
            src[x * WIDE : x * WIDE + HALO, :] = source_left[k, x]
            src[x * WIDE + WIDE - HALO : (x + 1) * WIDE, :] = source_right[k, x]
            if x < HALO:
                middle = source_up[k, x]
            elif x < HALO + TILE:
                middle = source_ref[k, x - HALO]
            else:
                middle = source_down[k, x - HALO - TILE]
            src[x * WIDE + HALO : x * WIDE + HALO + TILE, :] = middle
    lane = lax.broadcasted_iota(jnp.int32, (WIDE, LANES), 1)
    first, last = lane == 0, lane == LANES - 1

    def advance(a_m, a_e, b_m, b_e, s):
        for x in range(s + 1, WIDE - 1 - s):
            r = x * WIDE
            at = lambda off: pl.ds(r + pad + off, WIDE)
            own = pl.ds(r, WIDE)
            m, e = a_m[at(0), :], a_e[at(0), :]
            roll = lambda v, d: pltpu.roll(v, d % LANES, 1)
            mr, er, ml, el = roll(m, 1), roll(e, 1), roll(m, -1), roll(e, -1)
            sides = (
                (a_m, b_m, m, jnp.where(first, er, mr) + jnp.where(last, el, ml), 1, src_m),
                (a_e, b_e, e, jnp.where(first, mr, er) + jnp.where(last, ml, el), 3, src_e),
            )
            for a, b, v, beside, d, src in sides:
                beside = beside + (a[at(-WIDE), :] + a[at(WIDE), :])
                beside = beside + (a[at(-1), :] + a[at(1), :])
                b[at(0), :] = v + start_ref[d, own, :] * (beside - 6.0 * v) + src[own, :]
        for x in range(TILE):
            r = pad + (x + HALO) * WIDE + HALO
            for h in range(2):
                snaps[x * 2 + h, 8 * s : 8 * s + 8, :] = b_m[r + 8 * h : r + 8 * h + 8, :]

    for s in range(0, STEPS, 2):
        if s == 0:
            next_m[...] = jnp.zeros_like(next_m)
            next_e[...] = jnp.zeros_like(next_e)
        advance(now_m, now_e, next_m, next_e, s)
        advance(next_m, next_e, now_m, now_e, s + 1)
    for x in range(TILE):
        for h in range(2):
            field_ref[x, 8 * h : 8 * h + 8, :] = snaps[x * 2 + h, 8 * (STEPS - 1) :, :]

    load.wait()
    acc[...] = jnp.zeros_like(acc)
    tall = 8 * HIST

    for i in range(TILE):
        x, h = (i // 2) * 2, i % 2
        new = [snaps[(x + e) * 2 + h] for e in range(2)]
        old = [
            past[:, x + e, h * 8 : h * 8 + 8, :].reshape(tall, LANES)
            for e in range(2)
        ]
        new_high, new_low = split(jnp.concatenate(new, axis=1))
        old_high, old_low = split(jnp.concatenate(old, axis=1))
        right = jnp.concatenate([new_high, new_low], axis=0)
        acc[0:tall, :] += dot_nt(old_high, right) + dot_nt(old_low, right)
        acc[tall:, :] += dot_nt(new_high, right) + dot_nt(new_low, right)
    y = lax.broadcasted_iota(jnp.int32, acc.shape, 0) % 8
    y_new = lax.broadcasted_iota(jnp.int32, acc.shape, 1) % 8
    products = jnp.where(y == y_new, acc[...], 0.0).reshape(SNAPS, 8, 2 * 8 * STEPS).sum(axis=1)
    snap_of = lambda shape, dim: (lax.broadcasted_iota(jnp.int32, shape, dim) % 64) // 8
    wide, tallest = (2 * 8 * STEPS, SNAPS), (STEPS, 2 * 8 * STEPS)
    pick = snap_of(wide, 0) == lax.broadcasted_iota(jnp.int32, wide, 1) - HIST
    right = jnp.dot(
        products,
        jnp.where(pick, 1.0, 0.0),
        precision=lax.Precision.HIGHEST,
        preferred_element_type=f32,
    )
    pick = snap_of(tallest, 1) == lax.broadcasted_iota(jnp.int32, tallest, 0)
    low = dot_nt(jnp.where(pick, 1.0, 0.0), products, lax.Precision.HIGHEST)
    upper = past_gram[...] + right[:HIST]
    for f in range(rows_ref.shape[0] // SNAPS):
        rows_ref[f * SNAPS : f * SNAPS + HIST, :] = upper
        rows_ref[f * SNAPS + HIST : (f + 1) * SNAPS, :] = low


def up_chain(axis):
    count = lax.axis_size(axis)
    return [(i, i + 1) for i in range(count - 1)]


def down_chain(axis):
    count = lax.axis_size(axis)
    return [(i + 1, i) for i in range(count - 1)]


def beyond(cells):
    after = lax.ppermute(cells, "fluid", down_chain("fluid"))
    before = lax.ppermute(cells, "fluid", up_chain("fluid"))
    lane = lax.broadcasted_iota(jnp.int32, cells.shape, cells.ndim - 1)
    return jnp.where(lane < LANES // 2, after, before)


def slabs(cells):
    up = lax.ppermute(cells[:, TILE - HALO :], SX, up_chain(SX))
    down = lax.ppermute(cells[:, :HALO], SX, down_chain(SX))
    tall = jnp.concatenate([up, cells, down], axis=1)
    left = lax.ppermute(tall[:, :, TILE - HALO :], "sy", up_chain("sy"))
    right = lax.ppermute(tall[:, :, :HALO], "sy", down_chain("sy"))
    return up, down, tall, left, right


def whole(shape):
    return pl.BlockSpec(shape, lambda *_: (0,) * len(shape))


def local(
    opening_conductor_warmth,
    cellwise_diffusivity,
    previous_thermal_states,
    boundary_heat_rate_pieces,
    receiving_processor_per_piece,
    boundary_line_position_in_tile,
    piece_to_solid_line_mapping,
):
    blocks = boundary_heat_rate_pieces.shape[0]
    vmem = pl.BlockSpec(memory_space=pltpu.VMEM)
    smem = pl.BlockSpec(memory_space=pltpu.SMEM)
    limit = pltpu.CompilerParams(vmem_limit_bytes=48 * 1024 * 1024)

    with jax.named_scope("rank"):
        shift = (lax.axis_index("sy") % 4 * SLOTS).astype(jnp.int32).reshape(1)
        slots, labels = pl.pallas_call(
            rank_kernel,
            out_shape=(
                jax.ShapeDtypeStruct((1, blocks), jnp.int32),
                jax.ShapeDtypeStruct((CHUNK, LANES), f32),
            ),
            in_specs=[smem, vmem, vmem],
            out_specs=(vmem, vmem),
            compiler_params=limit,
        )(shift, receiving_processor_per_piece.T, boundary_line_position_in_tile.T)

    with jax.named_scope("pack"):
        packed = pl.pallas_call(
            pack_kernel,
            out_shape=jax.ShapeDtypeStruct((PEERS * PEER_ROWS, LANES), f32),
            in_specs=[smem, vmem, vmem],
            out_specs=vmem,
            compiler_params=limit,
        )(slots, boundary_heat_rate_pieces, labels)

    with jax.named_scope("exchange"):
        packed, states = lax.optimization_barrier((packed, previous_thermal_states))
        received = lax.all_to_all(
            packed.reshape(PEERS, PEER_ROWS, LANES), PLANE, split_axis=0, concat_axis=0, tiled=True
        )

    with jax.named_scope("history"):
        flat = states.reshape(HIST, -1)
        cells = float(flat.shape[1] * lax.axis_size(ALL))
        past_gram = jnp.dot(
            flat, flat.T, precision=lax.Precision.HIGHEST, preferred_element_type=f32
        )
        past_gram = jnp.pad(past_gram, ((0, 0), (0, STEPS)))

    with jax.named_scope("early_halo"):
        past_gram, pair = lax.optimization_barrier((past_gram, opening_conductor_warmth))
        pair = jnp.stack([pair, rate_step * cellwise_diffusivity])
        pair = jnp.concatenate([pair, beyond(pair)])
        _, _, tall, left, right = slabs(pair)
        start = jnp.concatenate([left, tall, right], axis=2).reshape(4, WIDE * WIDE, LANES)

    with jax.named_scope("deposit"):
        received, past_gram = lax.optimization_barrier((received, past_gram))
        mine = lax.axis_index("sxq").astype(jnp.int32).reshape(1)

        def deposit(ahead):
            return pl.pallas_call(
                functools.partial(deposit_kernel, ahead),
                out_shape=jax.ShapeDtypeStruct((LINES, LANES), f32),
                grid_spec=pltpu.PrefetchScalarGridSpec(
                    num_scalar_prefetch=1,
                    grid=(1,),
                    in_specs=[
                        pl.BlockSpec(
                            (PEERS, SLOTS, LANES), lambda _, quad: (0, (quad[0] + ahead) % QUADS, 0)
                        ),
                        pl.BlockSpec((PEERS, 8, LANES), lambda _, quad: (0, QUADS * SLOTS // 8, 0)),
                        whole((LANES, LANES)),
                    ],
                    out_specs=whole((LINES, LANES)),
                ),
                compiler_params=limit,
            )(mine, received, received, piece_to_solid_line_mapping)

        source = None
        for k in (2, 1, 3, 0):
            part = deposit(k)
            if k:
                part = lax.ppermute(part, "sxq", [(i, (i + k) % QUADS) for i in range(QUADS)])
            source = part if source is None else source + part
        source = source.reshape(1, TILE, TILE, LANES)

    with jax.named_scope("source_halo"):
        source = jnp.concatenate([source, beyond(source)])
        up, down, _, left, right = slabs(source)

    with jax.named_scope("steps"):
        rows = lax.axis_size("fluid") * SNAPS
        grid_rows = WIDE * WIDE
        buffer = pltpu.VMEM((grid_rows + 2 * WIDE, LANES), f32)
        field, gram_rows = pl.pallas_call(
            step_kernel,
            out_shape=(
                jax.ShapeDtypeStruct((TILE, TILE, LANES), f32),
                jax.ShapeDtypeStruct((rows, SNAPS), f32),
            ),
            in_specs=[vmem] * 7 + [pl.BlockSpec(memory_space=pl.ANY)],
            out_specs=(vmem, vmem),
            scratch_shapes=[
                buffer,
                buffer,
                buffer,
                buffer,
                pltpu.VMEM((grid_rows, LANES), f32),
                pltpu.VMEM((grid_rows, LANES), f32),
                pltpu.VMEM((TILE * 2, 8 * STEPS, LANES), f32),
                pltpu.VMEM((HIST, TILE, TILE, LANES), f32),
                pltpu.VMEM((8 * SNAPS, 2 * 8 * STEPS), f32),
                pltpu.SemaphoreType.DMA,
            ],
            compiler_params=limit,
        )(start, source, up, down, left, right, past_gram, previous_thermal_states)

    with jax.named_scope("gram_sum"):
        shares = lax.all_to_all(gram_rows, ALL, split_axis=0, concat_axis=0, tiled=True)
        inner_product_matrix = jnp.sum(shares, axis=0, keepdims=True) / cells
    return field, inner_product_matrix


def solution(mesh):
    fluid, sx, sy = (mesh.shape[name] for name in ("fluid", "sx", "sy"))
    inner = Mesh(mesh.devices.reshape(fluid, sx // 2, 2, sy), ALL)
    cell = P(SX, "sy", "fluid")
    wall = P(ALL, None)
    return jax.shard_map(
        local,
        mesh=inner,
        in_specs=(cell, cell, P(None, SX, "sy", "fluid"), wall, wall, wall, P()),
        out_specs=(cell, P((*SX, "sy"), None)),
        check_vma=False,
    )
```

```python
import functools

import jax
import jax.numpy as jnp
from jax import lax
from jax.experimental import pallas as pl
from jax.experimental.pallas import tpu as pltpu
from jax.sharding import Mesh
from jax.sharding import PartitionSpec as P

STEPS = 8
HALO = 8
HIST = 56
SNAPS = HIST + STEPS
SLOTS = 32
LINES = 256
LANES = 128
QUADS = 4
PEERS = 64
PEER_ROWS = QUADS * SLOTS + 8
CHUNK = 256
TILE = 16
WIDE = TILE + 2 * HALO

rate_step = 0.16
source_gain = 0.1

SX = ("sxq", "sxp")
PLANE = ("fluid", "sxp", "sy")
ALL = ("fluid", "sxq", "sxp", "sy")

f32 = jnp.float32
bf16 = jnp.bfloat16

LIMIT = pltpu.CompilerParams(vmem_limit_bytes=32 * 1024 * 1024)
FULL = pltpu.CompilerParams(vmem_limit_bytes=60 * 1024 * 1024)


def dot_nt(a, b, precision=None):
    return lax.dot_general(
        a, b, (((1,), (1,)), ((), ())), precision=precision, preferred_element_type=f32
    )


def split(x):
    high = x.astype(bf16)
    return high, (x - high.astype(f32)).astype(bf16)


def pack_kernel(
    shift_ref,
    owner_hbm,
    line_hbm,
    blocks_hbm,
    out_ref,
    owner_ref,
    line_ref,
    blocks_ref,
    slot_ref,
    slot_smem,
    sems,
):
    loads = [
        pltpu.make_async_copy(owner_hbm, owner_ref, sems.at[0]),
        pltpu.make_async_copy(line_hbm, line_ref, sems.at[1]),
        pltpu.make_async_copy(blocks_hbm, blocks_ref, sems.at[2]),
    ]
    for load in loads:
        load.start()
    out_ref[...] = jnp.zeros_like(out_ref)

    rows = lax.broadcasted_iota(jnp.int32, (CHUNK, CHUNK), 0)
    cols = lax.broadcasted_iota(jnp.int32, (CHUNK, CHUNK), 1)
    earlier = jnp.where(rows < cols, 1.0, 0.0).astype(bf16)
    places = lax.broadcasted_iota(jnp.int32, (LANES, CHUNK), 0)
    shift = shift_ref[0]
    carry = jnp.zeros((CHUNK, 1), f32)
    labels = jnp.zeros((CHUNK, LANES), f32)
    loads[0].wait()
    loads[1].wait()
    for c in range(0, owner_ref.shape[1], CHUNK):
        owner = owner_ref[:, c : c + CHUNK]
        fluid, sx, sy = owner >> 6, (owner >> 3) & 7, owner & 7
        peer = (fluid * 2 + (sx & 1)) * 8 + sy
        quad = sx >> 1
        match = rows == peer * QUADS + quad
        hit = jnp.where(match, 1.0, 0.0)
        hit16 = hit.astype(bf16)
        before = jnp.dot(hit16, earlier, preferred_element_type=f32)
        rank = jnp.sum(jnp.where(match, before + carry, 0.0), axis=0, keepdims=True)
        carry = carry + (before[:, CHUNK - 1 :] + hit[:, CHUNK - 1 :])
        rank = rank.astype(jnp.int32)
        slot_ref[:, c : c + CHUNK] = peer * PEER_ROWS + quad * SLOTS + rank
        value = (line_ref[:, c : c + CHUNK] + 1).astype(f32)
        spread = jnp.where(places == rank + shift, value, 0.0).astype(bf16)
        labels = labels + dot_nt(hit16, spread)
    to_smem = pltpu.make_async_copy(slot_ref, slot_smem, sems.at[3])
    to_smem.start()
    for g in range(PEERS):
        at = g * PEER_ROWS + QUADS * SLOTS
        out_ref[at : at + QUADS, :] = labels[QUADS * g : QUADS * (g + 1)]
    to_smem.wait()
    loads[2].wait()

    step = 64

    def place(i, _):
        base = pl.multiple_of(i * step, step)
        for t in range(step):
            out_ref[pl.ds(slot_smem[0, base + t], 1), :] = blocks_ref[pl.ds(base + t, 1), :]
        return 0

    lax.fori_loop(0, blocks_ref.shape[0] // step, place, 0)


def quad_step(ahead, step):
    value = ahead[0]
    for n in range(1, len(ahead)):
        value = jnp.where(step == n, ahead[n], value)
    return value


def deposit_kernel(ahead, quad_ref, block_ref, label_ref, map_ref, *out_refs):
    step = pl.program_id(0)
    quad = (quad_ref[0] + quad_step(ahead, step)) % QUADS
    lines = lax.broadcasted_iota(jnp.int32, (LINES, LANES), 0).astype(f32) + 1.0
    labels = label_ref[:, pl.ds(quad, 1), :].reshape(PEERS // 4, 4, LANES).sum(axis=1)
    total = jnp.zeros((LINES, 2 * LANES), f32)
    for g in range(PEERS // 8):
        marks = [
            jnp.where(lines == labels[h : h + 1], 1.0, 0.0).astype(bf16)
            for h in (2 * g, 2 * g + 1)
        ]
        high, low = split(block_ref[8 * g : 8 * g + 8].reshape(8 * SLOTS, LANES))
        total = total + jnp.dot(
            jnp.concatenate(marks, axis=1),
            jnp.concatenate([high, low], axis=1),
            preferred_element_type=f32,
        )
    high, low = split(total[:, :LANES] + total[:, LANES:])
    map_high, map_low = split(map_ref[...])
    both = jnp.concatenate([map_high, map_low], axis=1)
    once = jnp.concatenate([map_high, jnp.zeros_like(map_low)], axis=1)
    mapped = jnp.dot(
        jnp.concatenate([high, low], axis=1),
        jnp.concatenate([both, once], axis=0),
        preferred_element_type=f32,
    )
    result = source_gain * (mapped[:, :LANES] + mapped[:, LANES:])
    for n, out_ref in enumerate(out_refs):

        @pl.when(step == n)
        def _():
            out_ref[...] = result


def cut_kernel(field_ref, rate_ref, *refs):
    sources, (tile_ref, last_ref, first_ref) = refs[:QUADS], refs[QUADS:]
    source = sources[0][...]
    for ref in sources[1:]:
        source = source + ref[...]
    source = source.reshape(TILE, TILE, LANES)
    for k, value in enumerate((field_ref[...], rate_step * rate_ref[...], source)):
        tile_ref[k] = value
        first_ref[k] = value[:HALO]
        last_ref[k] = value[TILE - HALO :]


def side_kernel(up_ref, tile_ref, down_ref, last_ref, first_ref):
    for at, ref in ((0, up_ref), (HALO, tile_ref), (HALO + TILE, down_ref)):
        rows = slice(at, at + ref.shape[1])
        first_ref[:, rows] = ref[:, :, :HALO, :]
        last_ref[:, rows] = ref[:, :, TILE - HALO :, :]


def widen_kernel(up_ref, tile_ref, down_ref, left_ref, right_ref, wide_ref, low_ref, high_ref):
    for k in range(wide_ref.shape[0]):
        for at, ref in ((0, up_ref), (HALO, tile_ref), (HALO + TILE, down_ref)):
            for n in range(ref.shape[1]):
                x = at + n
                r = x * WIDE
                wide_ref[k, r : r + HALO, :] = left_ref[k, x]
                wide_ref[k, r + HALO : r + HALO + TILE, :] = ref[k, n]
                wide_ref[k, r + HALO + TILE : r + WIDE, :] = right_ref[k, x]
        for r in range(0, WIDE * WIDE, LANES):
            turned = wide_ref[k, r : r + LANES, :].T
            low_ref[k, :, r : r + LANES] = turned[:HALO]
            high_ref[k, :, r : r + LANES] = turned[LANES - HALO :]


def step_kernel(
    wide_ref,
    before_ref,
    after_ref,
    past_gram,
    past,
    field_ref,
    rows_ref,
    now_m,
    now_e,
    next_m,
    next_e,
    rate_e,
    src_e,
    snaps,
    acc,
):
    pad = WIDE
    count = WIDE * WIDE
    for now in (now_m, now_e, next_m, next_e):
        now[...] = jnp.zeros_like(now)
    now_m[pad : pad + count, :] = wide_ref[0]
    none = jnp.zeros((LANES - 2 * HALO, LANES), f32)
    for r in range(0, count, LANES):
        own = slice(r, r + LANES)
        for k, (to, off) in enumerate(((now_e, pad), (rate_e, 0), (src_e, 0))):
            lanes = jnp.concatenate([after_ref[k, :, own], none, before_ref[k, :, own]], axis=0)
            to[off + r : off + r + LANES, :] = lanes.T
    lane = lax.broadcasted_iota(jnp.int32, (WIDE, LANES), 1)
    first, last = lane == 0, lane == LANES - 1

    def advance(a_m, a_e, b_m, b_e, s):
        for x in range(s + 1, WIDE - 1 - s):
            r = x * WIDE
            at = lambda off: pl.ds(r + pad + off, WIDE)
            own = pl.ds(r, WIDE)
            m, e = a_m[at(0), :], a_e[at(0), :]
            roll = lambda v, d: pltpu.roll(v, d % LANES, 1)
            mr, er, ml, el = roll(m, 1), roll(e, 1), roll(m, -1), roll(e, -1)
            sides = (
                (a_m, b_m, m, jnp.where(first, er, mr) + jnp.where(last, el, ml)),
                (a_e, b_e, e, jnp.where(first, mr, er) + jnp.where(last, ml, el)),
            )
            rates = (wide_ref[1, own, :], rate_e[own, :])
            sources = (wide_ref[2, own, :], src_e[own, :])
            for (a, b, v, beside), rate, src in zip(sides, rates, sources):
                beside = beside + (a[at(-WIDE), :] + a[at(WIDE), :])
                beside = beside + (a[at(-1), :] + a[at(1), :])
                b[at(0), :] = v + rate * (beside - 6.0 * v) + src
        for x in range(TILE):
            r = pad + (x + HALO) * WIDE + HALO
            for h in range(2):
                snaps[x * 2 + h, 8 * s : 8 * s + 8, :] = b_m[r + 8 * h : r + 8 * h + 8, :]

    for s in range(0, STEPS, 2):
        advance(now_m, now_e, next_m, next_e, s)
        advance(next_m, next_e, now_m, now_e, s + 1)
    for x in range(TILE):
        for h in range(2):
            field_ref[x, 8 * h : 8 * h + 8, :] = snaps[x * 2 + h, 8 * (STEPS - 1) :, :]

    acc[...] = jnp.zeros_like(acc)
    tall = 8 * HIST

    for i in range(TILE):
        x, h = (i // 2) * 2, i % 2
        new = [snaps[(x + e) * 2 + h] for e in range(2)]
        old = [
            past[:, x + e, h * 8 : h * 8 + 8, :].reshape(tall, LANES)
            for e in range(2)
        ]
        new_high, new_low = split(jnp.concatenate(new, axis=1))
        old_high, old_low = split(jnp.concatenate(old, axis=1))
        right = jnp.concatenate([new_high, new_low], axis=0)
        acc[0:tall, :] += dot_nt(old_high, right) + dot_nt(old_low, right)
        acc[tall:, :] += dot_nt(new_high, right) + dot_nt(new_low, right)
    y = lax.broadcasted_iota(jnp.int32, acc.shape, 0) % 8
    y_new = lax.broadcasted_iota(jnp.int32, acc.shape, 1) % 8
    products = jnp.where(y == y_new, acc[...], 0.0).reshape(SNAPS, 8, 2 * 8 * STEPS).sum(axis=1)
    snap_of = lambda shape, dim: (lax.broadcasted_iota(jnp.int32, shape, dim) % 64) // 8
    wide, tallest = (2 * 8 * STEPS, SNAPS), (STEPS, 2 * 8 * STEPS)
    pick = snap_of(wide, 0) == lax.broadcasted_iota(jnp.int32, wide, 1) - HIST
    right = jnp.dot(
        products,
        jnp.where(pick, 1.0, 0.0),
        precision=lax.Precision.HIGHEST,
        preferred_element_type=f32,
    )
    pick = snap_of(tallest, 1) == lax.broadcasted_iota(jnp.int32, tallest, 0)
    low = dot_nt(jnp.where(pick, 1.0, 0.0), products, lax.Precision.HIGHEST)
    upper = past_gram[...] + right[:HIST]
    for f in range(rows_ref.shape[0] // SNAPS):
        rows_ref[f * SNAPS : f * SNAPS + HIST, :] = upper
        rows_ref[f * SNAPS + HIST : (f + 1) * SNAPS, :] = low


def up_chain(axis):
    count = lax.axis_size(axis)
    return [(i, i + 1) for i in range(count - 1)]


def down_chain(axis):
    count = lax.axis_size(axis)
    return [(i + 1, i) for i in range(count - 1)]


def stack(*shape):
    return jax.ShapeDtypeStruct((3, *shape), f32)


def in_vmem(kernel, out_shape, *args):
    vmem = pl.BlockSpec(memory_space=pltpu.VMEM)
    return pl.pallas_call(
        kernel,
        out_shape=out_shape,
        in_specs=[vmem] * len(args),
        out_specs=[vmem] * len(out_shape),
        compiler_params=LIMIT,
    )(*args)


def widened(field, rate, parts):
    half = stack(HALO, TILE, LANES)
    tile, last, first = in_vmem(
        cut_kernel, (stack(TILE, TILE, LANES), half, half), field, rate, *parts
    )
    up = lax.ppermute(last, SX, up_chain(SX))
    down = lax.ppermute(first, SX, down_chain(SX))
    half = stack(WIDE, HALO, LANES)
    last, first = in_vmem(side_kernel, (half, half), up, tile, down)
    left = lax.ppermute(last, "sy", up_chain("sy"))
    right = lax.ppermute(first, "sy", down_chain("sy"))
    edge = stack(HALO, WIDE * WIDE)
    wide, low, high = in_vmem(
        widen_kernel, (stack(WIDE * WIDE, LANES), edge, edge), up, tile, down, left, right
    )
    before = lax.ppermute(high, "fluid", up_chain("fluid"))
    after = lax.ppermute(low, "fluid", down_chain("fluid"))
    return wide, before, after


def whole(shape):
    return pl.BlockSpec(shape, lambda *_: (0,) * len(shape))


def local(
    opening_conductor_warmth,
    cellwise_diffusivity,
    previous_thermal_states,
    boundary_heat_rate_pieces,
    receiving_processor_per_piece,
    boundary_line_position_in_tile,
    piece_to_solid_line_mapping,
):
    blocks = boundary_heat_rate_pieces.shape[0]
    vmem = pl.BlockSpec(memory_space=pltpu.VMEM)
    smem = pl.BlockSpec(memory_space=pltpu.SMEM)
    hbm = pl.BlockSpec(memory_space=pltpu.HBM)

    with jax.named_scope("pack"):
        shift = (lax.axis_index("sy") % 4 * SLOTS).astype(jnp.int32).reshape(1)
        packed = pl.pallas_call(
            pack_kernel,
            out_shape=jax.ShapeDtypeStruct((PEERS * PEER_ROWS, LANES), f32),
            in_specs=[smem] + [hbm] * 3,
            out_specs=vmem,
            scratch_shapes=[
                pltpu.VMEM((1, blocks), jnp.int32),
                pltpu.VMEM((1, blocks), jnp.int32),
                pltpu.VMEM((blocks, LANES), f32),
                pltpu.VMEM((1, blocks), jnp.int32),
                pltpu.SMEM((1, blocks), jnp.int32),
                pltpu.SemaphoreType.DMA((4,)),
            ],
            compiler_params=FULL,
        )(
            shift,
            receiving_processor_per_piece.T,
            boundary_line_position_in_tile.T,
            boundary_heat_rate_pieces,
        )

    with jax.named_scope("exchange"):
        packed, states = lax.optimization_barrier((packed, previous_thermal_states))
        received = lax.all_to_all(
            packed.reshape(PEERS, PEER_ROWS, LANES), PLANE, split_axis=0, concat_axis=0, tiled=True
        )

    with jax.named_scope("history"):
        flat = states.reshape(HIST, -1)
        cells = float(flat.shape[1] * lax.axis_size(ALL))
        past_gram = jnp.dot(
            flat, flat.T, precision=lax.Precision.HIGHEST, preferred_element_type=f32
        )
        past_gram = jnp.pad(past_gram, ((0, 0), (0, STEPS)))

    with jax.named_scope("deposit"):
        received, past_gram = lax.optimization_barrier((received, past_gram))
        mine = lax.axis_index("sxq").astype(jnp.int32).reshape(1)

        def deposit(*ahead):
            quad_of = lambda step, quad: (quad[0] + quad_step(ahead, step)) % QUADS
            return pl.pallas_call(
                functools.partial(deposit_kernel, ahead),
                out_shape=[jax.ShapeDtypeStruct((LINES, LANES), f32)] * len(ahead),
                grid_spec=pltpu.PrefetchScalarGridSpec(
                    num_scalar_prefetch=1,
                    grid=(len(ahead),),
                    in_specs=[
                        pl.BlockSpec(
                            (PEERS, SLOTS, LANES), lambda step, quad: (0, quad_of(step, quad), 0)
                        ),
                        pl.BlockSpec((PEERS, 8, LANES), lambda *_: (0, QUADS * SLOTS // 8, 0)),
                        whole((LANES, LANES)),
                    ],
                    out_specs=[whole((LINES, LANES))] * len(ahead),
                ),
                compiler_params=LIMIT,
            )(mine, received, received, piece_to_solid_line_mapping)

        ahead = (2, 1, 3)
        parts = [
            lax.ppermute(part, "sxq", [(i, (i + k) % QUADS) for i in range(QUADS)])
            for k, part in zip(ahead, deposit(*ahead))
        ]
        parts = [*deposit(0), *parts]

    with jax.named_scope("halo"):
        wide, before, after = widened(opening_conductor_warmth, cellwise_diffusivity, parts)

    with jax.named_scope("steps"):
        rows = lax.axis_size("fluid") * SNAPS
        grid_rows = WIDE * WIDE
        buffer = pltpu.VMEM((grid_rows + 2 * WIDE, LANES), f32)
        field, gram_rows = pl.pallas_call(
            step_kernel,
            out_shape=(
                jax.ShapeDtypeStruct((TILE, TILE, LANES), f32),
                jax.ShapeDtypeStruct((rows, SNAPS), f32),
            ),
            in_specs=[vmem] * 5,
            out_specs=(vmem, vmem),
            scratch_shapes=[
                buffer,
                buffer,
                buffer,
                buffer,
                pltpu.VMEM((grid_rows, LANES), f32),
                pltpu.VMEM((grid_rows, LANES), f32),
                pltpu.VMEM((TILE * 2, 8 * STEPS, LANES), f32),
                pltpu.VMEM((8 * SNAPS, 2 * 8 * STEPS), f32),
            ],
            compiler_params=LIMIT,
        )(wide, before, after, past_gram, previous_thermal_states)

    with jax.named_scope("gram_sum"):
        shares = lax.all_to_all(gram_rows, ALL, split_axis=0, concat_axis=0, tiled=True)
        inner_product_matrix = jnp.sum(shares, axis=0, keepdims=True) / cells
    return field, inner_product_matrix


def solution(mesh):
    fluid, sx, sy = (mesh.shape[name] for name in ("fluid", "sx", "sy"))
    inner = Mesh(mesh.devices.reshape(fluid, sx // 2, 2, sy), ALL)
    cell = P(SX, "sy", "fluid")
    wall = P(ALL, None)
    return jax.shard_map(
        local,
        mesh=inner,
        in_specs=(cell, cell, P(None, SX, "sy", "fluid"), wall, wall, wall, P()),
        out_specs=(cell, P((*SX, "sy"), None)),
        check_vma=False,
    )
```

```python
import functools

import jax
import jax.numpy as jnp
from jax import lax
from jax.experimental import pallas as pl
from jax.experimental.pallas import tpu as pltpu
from jax.sharding import Mesh
from jax.sharding import PartitionSpec as P

STEPS = 8
HALO = 8
HIST = 56
SNAPS = HIST + STEPS
SLOTS = 32
LINES = 256
LANES = 128
QUADS = 4
PEERS = 64
PEER_ROWS = QUADS * SLOTS + 1
ORDER = (2, 1, 3, 0)
CHUNK = 256
TILE = 16
WIDE = TILE + 2 * HALO

rate_step = 0.16
source_gain = 0.1

SX = ("sxq", "sxp")
PLANE = ("fluid", "sxp", "sy")
ALL = ("fluid", "sxq", "sxp", "sy")

f32 = jnp.float32
bf16 = jnp.bfloat16

LIMIT = pltpu.CompilerParams(vmem_limit_bytes=32 * 1024 * 1024)
LOADS = 4
FULL = pltpu.CompilerParams(vmem_limit_bytes=60 * 1024 * 1024)


def dot_nt(a, b, precision=None):
    return lax.dot_general(
        a, b, (((1,), (1,)), ((), ())), precision=precision, preferred_element_type=f32
    )


def split(x):
    high = x.astype(bf16)
    return high, (x - high.astype(f32)).astype(bf16)


def pack_kernel(
    mine_ref,
    owner_hbm,
    line_hbm,
    blocks_hbm,
    out_ref,
    owner_ref,
    line_ref,
    blocks_ref,
    slot_ref,
    slot_smem,
    sems,
):
    loads = [
        pltpu.make_async_copy(owner_hbm, owner_ref, sems.at[0]),
        pltpu.make_async_copy(line_hbm, line_ref, sems.at[1]),
        pltpu.make_async_copy(blocks_hbm, blocks_ref, sems.at[2]),
    ]
    for load in loads:
        load.start()
    out_ref[...] = jnp.zeros_like(out_ref)

    rows = lax.broadcasted_iota(jnp.int32, (CHUNK, CHUNK), 0)
    cols = lax.broadcasted_iota(jnp.int32, (CHUNK, CHUNK), 1)
    earlier = jnp.where(rows < cols, 1.0, 0.0).astype(bf16)
    spots = lax.broadcasted_iota(jnp.int32, (LANES, CHUNK), 0)
    peers = lax.broadcasted_iota(jnp.int32, (PEERS, CHUNK), 0)
    my_quad, my_turn = mine_ref[0] >> 2, mine_ref[0] & 3
    carry = jnp.zeros((CHUNK, 1), f32)
    labels = jnp.zeros((PEERS, LANES), f32)
    loads[0].wait()
    loads[1].wait()
    span = owner_ref.shape[1] // 2
    copies = []
    for begin in (0, span):
        for c in range(begin, begin + span, CHUNK):
            owner = owner_ref[:, c : c + CHUNK]
            fluid, sx, sy = owner >> 6, (owner >> 3) & 7, owner & 7
            peer = (fluid * 2 + (sx & 1)) * 8 + sy
            ahead = ((sx >> 1) - my_quad) & 3
            place = jnp.where(ahead == 0, 3, jnp.where(ahead == 1, 1, jnp.where(ahead == 2, 0, 2)))
            match = rows == peer * QUADS + place
            hit = jnp.where(match, 1.0, 0.0)
            hit16 = hit.astype(bf16)
            before = jnp.dot(hit16, earlier, preferred_element_type=f32)
            rank = jnp.sum(jnp.where(match, before + carry, 0.0), axis=0, keepdims=True)
            carry = carry + (before[:, CHUNK - 1 :] + hit[:, CHUNK - 1 :])
            rank = rank.astype(jnp.int32)
            slot_ref[:, c : c + CHUNK] = peer * PEER_ROWS + place * SLOTS + rank
            value = (line_ref[:, c : c + CHUNK] + 1).astype(f32)
            spot = ((place + my_turn) & 3) * SLOTS + rank
            spread = jnp.where(spots == spot, value, 0.0).astype(bf16)
            labels = labels + dot_nt(jnp.where(peers == peer, 1.0, 0.0).astype(bf16), spread)
        window = slice(begin, begin + span)
        copies.append(
            pltpu.make_async_copy(
                slot_ref.at[:, window], slot_smem.at[:, window], sems.at[3 + begin // span]
            )
        )
        copies[-1].start()
    for g in range(PEERS):
        at = g * PEER_ROWS + QUADS * SLOTS
        out_ref[at : at + 1, :] = labels[g : g + 1]
    loads[2].wait()
    step = 128
    for n, copy in enumerate(copies):
        copy.wait()

        def put(i, _):
            base = pl.multiple_of(n * span + i * step, step)
            for t in range(step):
                out_ref[pl.ds(slot_smem[0, base + t], 1), :] = blocks_ref[pl.ds(base + t, 1), :]
            return 0

        lax.fori_loop(0, span // step, put, 0)


def deposit_kernel(places, received_hbm, map_ref, *refs):
    outs, (values_ref, total_ref, sems) = refs[: len(places)], refs[len(places) :]
    rows = PEERS * PEER_ROWS // LOADS
    loads = [
        pltpu.make_async_copy(
            received_hbm.at[n * rows : (n + 1) * rows],
            values_ref.at[n * rows : (n + 1) * rows],
            sems.at[n],
        )
        for n in range(LOADS)
    ]
    for load in loads:
        load.start()
    lines = lax.broadcasted_iota(jnp.int32, (LINES, LANES), 0).astype(f32) + 1.0
    group = lax.broadcasted_iota(jnp.int32, (1, LANES), 1) // SLOTS

    def gathered(first, place):
        label, values = jnp.zeros((1, LANES), f32), [None] * 4
        for t in range(4):
            at = (first + t) * PEER_ROWS
            turn = (place + t) % 4
            row = values_ref[at + QUADS * SLOTS : at + PEER_ROWS, :]
            label = jnp.where(group == turn, row, label)
            values[turn] = values_ref[at + place * SLOTS : at + (place + 1) * SLOTS, :]
        return jnp.where(lines == label, 1.0, 0.0).astype(bf16), jnp.concatenate(values, axis=0)

    for n, load in enumerate(loads):
        load.wait()
        for first in range(n * PEERS // LOADS, (n + 1) * PEERS // LOADS, 8):
            for k, place in enumerate(places):
                marks, values = zip(gathered(first, place), gathered(first + 4, place))
                high, low = split(jnp.concatenate(values, axis=0))
                part = jnp.dot(
                    jnp.concatenate(marks, axis=1),
                    jnp.concatenate([high, low], axis=1),
                    preferred_element_type=f32,
                )
                total_ref[k] = part if first == 0 else total_ref[k] + part
    map_high, map_low = split(map_ref[...])
    both = jnp.concatenate([map_high, map_low], axis=1)
    once = jnp.concatenate([map_high, jnp.zeros_like(map_low)], axis=1)
    weights = jnp.concatenate([both, once], axis=0)
    for k, out_ref in enumerate(outs):
        high, low = split(total_ref[k, :, :LANES] + total_ref[k, :, LANES:])
        mapped = jnp.dot(
            jnp.concatenate([high, low], axis=1), weights, preferred_element_type=f32
        )
        out_ref[...] = source_gain * (mapped[:, :LANES] + mapped[:, LANES:])


def cut_kernel(field_ref, rate_ref, *refs):
    sources, (tile_ref, last_ref, first_ref) = refs[:QUADS], refs[QUADS:]
    source = sources[0][...]
    for ref in sources[1:]:
        source = source + ref[...]
    source = source.reshape(TILE, TILE, LANES)
    for k, value in enumerate((field_ref[...], rate_step * rate_ref[...], source)):
        tile_ref[k] = value
        first_ref[k] = value[:HALO]
        last_ref[k] = value[TILE - HALO :]


def side_kernel(up_ref, tile_ref, down_ref, last_ref, first_ref):
    for at, ref in ((0, up_ref), (HALO, tile_ref), (HALO + TILE, down_ref)):
        rows = slice(at, at + ref.shape[1])
        first_ref[:, rows] = ref[:, :, :HALO, :]
        last_ref[:, rows] = ref[:, :, TILE - HALO :, :]


def widen_kernel(up_ref, tile_ref, down_ref, left_ref, right_ref, wide_ref, low_ref, high_ref):
    for k in range(wide_ref.shape[0]):
        for at, ref in ((0, up_ref), (HALO, tile_ref), (HALO + TILE, down_ref)):
            for n in range(ref.shape[1]):
                x = at + n
                r = x * WIDE
                wide_ref[k, r : r + HALO, :] = left_ref[k, x]
                wide_ref[k, r + HALO : r + HALO + TILE, :] = ref[k, n]
                wide_ref[k, r + HALO + TILE : r + WIDE, :] = right_ref[k, x]
        for r in range(0, WIDE * WIDE, LANES):
            turned = wide_ref[k, r : r + LANES, :].T
            low_ref[k, :, r : r + LANES] = turned[:HALO]
            high_ref[k, :, r : r + LANES] = turned[LANES - HALO :]


def step_kernel(
    scale,
    wide_ref,
    before_ref,
    after_ref,
    past_gram,
    past,
    field_ref,
    rows_ref,
    now_m,
    now_e,
    next_m,
    next_e,
    rate_e,
    src_e,
    snaps,
    acc,
):
    pad = WIDE
    count = WIDE * WIDE
    for now in (now_m, now_e, next_m, next_e):
        now[...] = jnp.zeros_like(now)
    now_m[pad : pad + count, :] = wide_ref[0]
    none = jnp.zeros((LANES - 2 * HALO, LANES), f32)
    for r in range(0, count, LANES):
        own = slice(r, r + LANES)
        for k, (to, off) in enumerate(((now_e, pad), (rate_e, 0), (src_e, 0))):
            lanes = jnp.concatenate([after_ref[k, :, own], none, before_ref[k, :, own]], axis=0)
            to[off + r : off + r + LANES, :] = lanes.T

    def advance(a_m, a_e, b_m, b_e, s):
        alone = s == STEPS - 1
        begin, height = (HALO, TILE) if alone else (0, WIDE)
        lane = lax.broadcasted_iota(jnp.int32, (height, LANES), 1)
        first, last = lane == 0, lane == LANES - 1
        for x in range(s + 1, WIDE - 1 - s):
            r = x * WIDE + begin
            at = lambda off: pl.ds(r + pad + off, height)
            own = pl.ds(r, height)
            m, e = a_m[at(0), :], a_e[at(0), :]
            roll = lambda v, d: pltpu.roll(v, d % LANES, 1)
            mr, er, ml, el = roll(m, 1), roll(e, 1), roll(m, -1), roll(e, -1)
            sides = [
                (a_m, b_m, m, jnp.where(first, er, mr) + jnp.where(last, el, ml)),
                (a_e, b_e, e, jnp.where(first, mr, er) + jnp.where(last, ml, el)),
            ]
            rates = (wide_ref[1, own, :], rate_e[own, :])
            sources = (wide_ref[2, own, :], src_e[own, :])
            for (a, b, v, beside), rate, src in zip(sides[: 1 if alone else 2], rates, sources):
                beside = beside + (a[at(-WIDE), :] + a[at(WIDE), :])
                beside = beside + (a[at(-1), :] + a[at(1), :])
                b[at(0), :] = v + rate * (beside - 6.0 * v) + src
        for x in range(TILE):
            r = pad + (x + HALO) * WIDE + HALO
            for h in range(2):
                snaps[x * 2 + h, 8 * s : 8 * s + 8, :] = b_m[r + 8 * h : r + 8 * h + 8, :]

    for s in range(0, STEPS, 2):
        advance(now_m, now_e, next_m, next_e, s)
        advance(next_m, next_e, now_m, now_e, s + 1)
    for x in range(TILE):
        for h in range(2):
            field_ref[x, 8 * h : 8 * h + 8, :] = snaps[x * 2 + h, 8 * (STEPS - 1) :, :]

    acc[...] = jnp.zeros_like(acc)
    tall = 8 * HIST

    for i in range(TILE):
        x, h = (i // 2) * 2, i % 2
        new = [snaps[(x + e) * 2 + h] for e in range(2)]
        old = [
            past[:, x + e, h * 8 : h * 8 + 8, :].reshape(tall, LANES)
            for e in range(2)
        ]
        new_high, new_low = split(jnp.concatenate(new, axis=1))
        old_high, old_low = split(jnp.concatenate(old, axis=1))
        right = jnp.concatenate([new_high, new_low], axis=0)
        acc[0:tall, :] += dot_nt(old_high, right) + dot_nt(old_low, right)
        acc[tall:, :] += dot_nt(new_high, right) + dot_nt(new_low, right)
    y = lax.broadcasted_iota(jnp.int32, acc.shape, 0) % 8
    y_new = lax.broadcasted_iota(jnp.int32, acc.shape, 1) % 8
    products = jnp.where(y == y_new, acc[...], 0.0).reshape(SNAPS, 8, 2 * 8 * STEPS).sum(axis=1)
    snap_of = lambda shape, dim: (lax.broadcasted_iota(jnp.int32, shape, dim) % 64) // 8
    wide, tallest = (2 * 8 * STEPS, SNAPS), (STEPS, 2 * 8 * STEPS)
    pick = snap_of(wide, 0) == lax.broadcasted_iota(jnp.int32, wide, 1) - HIST
    right = jnp.dot(
        products,
        jnp.where(pick, 1.0, 0.0),
        precision=lax.Precision.HIGHEST,
        preferred_element_type=f32,
    )
    pick = snap_of(tallest, 1) == lax.broadcasted_iota(jnp.int32, tallest, 0)
    low = dot_nt(jnp.where(pick, 1.0, 0.0), products, lax.Precision.HIGHEST)
    upper = scale * (past_gram[...] + right[:HIST])
    low = scale * low
    for f in range(rows_ref.shape[0] // SNAPS):
        rows_ref[f * SNAPS : f * SNAPS + HIST, :] = upper
        rows_ref[f * SNAPS + HIST : (f + 1) * SNAPS, :] = low


def up_chain(axis):
    count = lax.axis_size(axis)
    return [(i, i + 1) for i in range(count - 1)]


def down_chain(axis):
    count = lax.axis_size(axis)
    return [(i + 1, i) for i in range(count - 1)]


def stack(*shape):
    return jax.ShapeDtypeStruct((3, *shape), f32)


def in_vmem(kernel, out_shape, *args):
    vmem = pl.BlockSpec(memory_space=pltpu.VMEM)
    return pl.pallas_call(
        kernel,
        out_shape=out_shape,
        in_specs=[vmem] * len(args),
        out_specs=[vmem] * len(out_shape),
        compiler_params=LIMIT,
    )(*args)


def widened(field, rate, parts):
    half = stack(HALO, TILE, LANES)
    tile, last, first = in_vmem(
        cut_kernel, (stack(TILE, TILE, LANES), half, half), field, rate, *parts
    )
    up = lax.ppermute(last, SX, up_chain(SX))
    down = lax.ppermute(first, SX, down_chain(SX))
    half = stack(WIDE, HALO, LANES)
    last, first = in_vmem(side_kernel, (half, half), up, tile, down)
    left = lax.ppermute(last, "sy", up_chain("sy"))
    right = lax.ppermute(first, "sy", down_chain("sy"))
    edge = stack(HALO, WIDE * WIDE)
    wide, low, high = in_vmem(
        widen_kernel, (stack(WIDE * WIDE, LANES), edge, edge), up, tile, down, left, right
    )
    before = lax.ppermute(high, "fluid", up_chain("fluid"))
    after = lax.ppermute(low, "fluid", down_chain("fluid"))
    return wide, before, after


def local(
    opening_conductor_warmth,
    cellwise_diffusivity,
    previous_thermal_states,
    boundary_heat_rate_pieces,
    receiving_processor_per_piece,
    boundary_line_position_in_tile,
    piece_to_solid_line_mapping,
):
    blocks = boundary_heat_rate_pieces.shape[0]
    vmem = pl.BlockSpec(memory_space=pltpu.VMEM)
    smem = pl.BlockSpec(memory_space=pltpu.SMEM)
    hbm = pl.BlockSpec(memory_space=pltpu.HBM)

    with jax.named_scope("pack"):
        mine = lax.axis_index("sxq") * 4 + lax.axis_index("sy") % 4
        mine = mine.astype(jnp.int32).reshape(1)
        packed = pl.pallas_call(
            pack_kernel,
            out_shape=jax.ShapeDtypeStruct((PEERS * PEER_ROWS, LANES), f32),
            in_specs=[smem] + [hbm] * 3,
            out_specs=vmem,
            scratch_shapes=[
                pltpu.VMEM((1, blocks), jnp.int32),
                pltpu.VMEM((1, blocks), jnp.int32),
                pltpu.VMEM((blocks, LANES), f32),
                pltpu.VMEM((1, blocks), jnp.int32),
                pltpu.SMEM((1, blocks), jnp.int32),
                pltpu.SemaphoreType.DMA((5,)),
            ],
            compiler_params=FULL,
        )(
            mine,
            receiving_processor_per_piece.T,
            boundary_line_position_in_tile.T,
            boundary_heat_rate_pieces,
        )

    with jax.named_scope("exchange"):
        packed, states = lax.optimization_barrier((packed, previous_thermal_states))
        received = lax.all_to_all(
            packed.reshape(PEERS * PEER_ROWS, 1, LANES), PLANE, split_axis=0, concat_axis=0, tiled=True
        )

    with jax.named_scope("history"):
        flat = states.reshape(HIST, -1)
        cells = float(flat.shape[1] * lax.axis_size(ALL))
        past_gram = jnp.dot(
            flat, flat.T, precision=lax.Precision.HIGHEST, preferred_element_type=f32
        )
        past_gram = jnp.pad(past_gram, ((0, 0), (0, STEPS)))

    with jax.named_scope("deposit"):
        received, past_gram = lax.optimization_barrier((received, past_gram))
        received = received.reshape(PEERS * PEER_ROWS, LANES)

        def deposit(*places):
            return pl.pallas_call(
                functools.partial(deposit_kernel, places),
                out_shape=[jax.ShapeDtypeStruct((LINES, LANES), f32)] * len(places),
                in_specs=[hbm, vmem],
                out_specs=[vmem] * len(places),
                scratch_shapes=[
                    pltpu.VMEM((PEERS * PEER_ROWS, LANES), f32),
                    pltpu.VMEM((len(places), LINES, 2 * LANES), f32),
                    pltpu.SemaphoreType.DMA((LOADS,)),
                ],
                compiler_params=LIMIT,
            )(received, piece_to_solid_line_mapping)

        parts = [
            lax.ppermute(part, "sxq", [(i, (i + k) % QUADS) for i in range(QUADS)])
            for k, part in zip(ORDER, deposit(0, 1, 2))
        ]
        parts = [*deposit(3), *parts]

    with jax.named_scope("halo"):
        wide, before, after = widened(opening_conductor_warmth, cellwise_diffusivity, parts)

    with jax.named_scope("steps"):
        rows = lax.axis_size("fluid") * SNAPS
        grid_rows = WIDE * WIDE
        buffer = pltpu.VMEM((grid_rows + 2 * WIDE, LANES), f32)
        field, gram_rows = pl.pallas_call(
            functools.partial(step_kernel, 1.0 / cells),
            out_shape=(
                jax.ShapeDtypeStruct((TILE, TILE, LANES), f32),
                jax.ShapeDtypeStruct((rows, SNAPS), f32),
            ),
            in_specs=[vmem] * 5,
            out_specs=(vmem, vmem),
            scratch_shapes=[
                buffer,
                buffer,
                buffer,
                buffer,
                pltpu.VMEM((grid_rows, LANES), f32),
                pltpu.VMEM((grid_rows, LANES), f32),
                pltpu.VMEM((TILE * 2, 8 * STEPS, LANES), f32),
                pltpu.VMEM((8 * SNAPS, 2 * 8 * STEPS), f32),
            ],
            compiler_params=LIMIT,
        )(wide, before, after, past_gram, previous_thermal_states)

    with jax.named_scope("gram_sum"):
        shares = lax.all_to_all(gram_rows, ALL, split_axis=0, concat_axis=0, tiled=True)
        inner_product_matrix = jnp.sum(shares, axis=0, keepdims=True)
    return field, inner_product_matrix


def solution(mesh):
    fluid, sx, sy = (mesh.shape[name] for name in ("fluid", "sx", "sy"))
    inner = Mesh(mesh.devices.reshape(fluid, sx // 2, 2, sy), ALL)
    cell = P(SX, "sy", "fluid")
    wall = P(ALL, None)
    return jax.shard_map(
        local,
        mesh=inner,
        in_specs=(cell, cell, P(None, SX, "sy", "fluid"), wall, wall, wall, P()),
        out_specs=(cell, P((*SX, "sy"), None)),
        check_vma=False,
    )
```
